512 devices in a mesh: ctx: 64 (over y, x, core), head: 8 (over z).
Axes of the slice: x: 4, y: 8, z: 8, core: 2. Of those that a mesh axis runs over, the one named last changes fastest.
Arguments:
- x_prompt: bfloat16 [32768, 4096], P('ctx', 'head'), may hold values from -6 to 6
- norm_gain: bfloat16 [4096], replicated, may hold values from 0.25 to 1.75
- key_weight: bfloat16 [4096, 4096], P('ctx', 'head'), may hold values from -0.09375 to 0.09375
- value_weight: bfloat16 [4096, 4096], P('ctx', 'head'), may hold values from -0.09375 to 0.09375
- cache_keys: bfloat16 [32768, 4096], P('ctx', 'head'), may hold values from -6 to 6
- cache_values: bfloat16 [32768, 4096], P('ctx', 'head'), may hold values from -6 to 6
- resp_queries: bfloat16 [512, 4096], P('ctx', 'head'), may hold values from -270 to 270
- resp_keys: bfloat16 [512, 4096], P('ctx', 'head'), may hold values from -6 to 6
- resp_values: bfloat16 [512, 4096], P('ctx', 'head'), may hold values from -6 to 6
- drift_ids: int32 [64, 4], replicated, may hold values from 0 to 3, as said below
- drift_count: int32 [64], replicated, may hold values from 0 to 4, as said below
Outputs:
- new_keys: bfloat16 [32768, 4096], P('ctx', 'head')
- new_values: bfloat16 [32768, 4096], P('ctx', 'head')
- attended: bfloat16 [512, 4096], P('ctx', 'head')
The draws below stay inside these ranges and needn't reach their ends.
Inputs may be any that keep to these rules, and one draw needn't show every extreme that they name: `drift_ids`: each row s holds distinct block numbers of shard s; entries at or beyond drift_count[s] are ignored. `drift_count`: some shard has exactly 4 drifted blocks.
All inputs are finite; a program needn't handle non-finite values.
Results may differ from the reference program's by a relative error of at most 0.0078.
Values may be sent and summed in bfloat16 or wider, within the bound.
No kernel may reach another device: no remote copies, remote signals or barrier semaphores. Data moves between devices by JAX's collectives and lax.ppermute only.
A program may use at most 64 MiB of HBM per device.

```python
import jax
import jax.numpy as jnp
from jax import lax

D = 4096
HEADS = 32
HD = 128
BLOCK = 128
SLOTS = 4
CTX_DEV = 512
RESP_DEV = 8
CTX = 32768
RESP = 512
N_CTX = 64


def draw_drift_ids(key, part):
    key = jax.random.fold_in(key, 11)
    keys = jax.random.split(key, N_CTX)
    order = jax.vmap(lambda k: jax.random.permutation(k, CTX_DEV // BLOCK))(keys)
    return order[:, :SLOTS].astype(jnp.int32)


def draw_drift_count(key, part):
    key = jax.random.fold_in(key, 12)
    first, second, third = jax.random.split(key, 3)
    lower = jnp.minimum(jax.random.randint(first, (N_CTX,), 0, SLOTS + 1), jax.random.randint(second, (N_CTX,), 0, SLOTS + 1))
    busiest = jax.random.randint(third, (), 0, N_CTX)
    return jnp.where(jnp.arange(N_CTX) == busiest, SLOTS, lower).astype(jnp.int32)


def draw_resp_queries(key, part):
    key = jax.random.fold_in(key, 13)
    first = jax.random.fold_in(key, 0)
    base = jnp.clip(jax.random.normal(first, (RESP, HEADS * HD), jnp.float32), -4.5, 4.5)
    return (base * 3.0).astype(jnp.bfloat16)


def steps_of(own_key, shape, shards, smallest, largest):
    level = 1.0
    for axis_at, shards_of in shards:
        steps = jax.random.uniform(jax.random.fold_in(jax.random.fold_in(own_key, 6), axis_at), (shards_of,), jnp.float32, smallest / len(shards), largest / len(shards))
        level = level * jnp.repeat(jnp.exp(steps), shape[axis_at] // shards_of).reshape((-1,) + (1,) * (len(shape) - 1 - axis_at))
    return level


def scatter_about(own_key, shape, width, bound, cuts=(), kind=jnp.bfloat16):
    loudness = steps_of(own_key, shape, cuts, -0.22, 0.18) if cuts else 1.0
    array = jax.random.normal(own_key, shape, jnp.float32) * width * loudness
    return jnp.minimum(jnp.maximum(array, -bound), bound).astype(kind)


def setup_inputs(seed: int = 0) -> dict:
    key_of = jax.random.split(jax.random.key(seed), 12)
    x_prompt = scatter_about(key_of[0], (CTX, D), 1.0, 6.0, ((0, 64), (1, 8)))
    norm_gain = jnp.clip(1.0 + 0.15 * jax.random.normal(key_of[1], (D,), jnp.float32), 0.25, 1.75).astype(jnp.bfloat16)
    key_weight = scatter_about(key_of[2], (D, HEADS * HD), D ** -0.5, 0.09375, ((0, 64), (1, 8)))
    value_weight = scatter_about(key_of[3], (D, HEADS * HD), D ** -0.5, 0.09375, ((0, 64), (1, 8)))
    cache_keys = scatter_about(key_of[4], (CTX, HEADS * HD), 1.0, 6.0, ((0, 64), (1, 8)))
    cache_values = scatter_about(key_of[5], (CTX, HEADS * HD), 1.0, 6.0, ((0, 64), (1, 8)))
    resp_queries = draw_resp_queries(jax.random.fold_in(key_of[11], 71), 0)
    resp_keys = scatter_about(key_of[7], (RESP, HEADS * HD), 1.0, 6.0, ((0, 64), (1, 8)))
    resp_values = scatter_about(key_of[8], (RESP, HEADS * HD), 1.0, 6.0, ((0, 64), (1, 8)))
    drift_ids = draw_drift_ids(jax.random.fold_in(key_of[11], 71), 0)
    drift_count = draw_drift_count(jax.random.fold_in(key_of[11], 71), 0)
    return dict(x_prompt=x_prompt, norm_gain=norm_gain, key_weight=key_weight, value_weight=value_weight, cache_keys=cache_keys, cache_values=cache_values, resp_queries=resp_queries, resp_keys=resp_keys, resp_values=resp_values, drift_ids=drift_ids, drift_count=drift_count)


eps = 1e-05

def normalize(rows, gain):
    values = rows.astype(jnp.float32)
    scale = lax.rsqrt(lax.optimization_barrier(jnp.mean(values * values, axis=1, keepdims=True)) + eps)
    return (values * scale * gain[None, :]).astype(jnp.bfloat16)

def reference(x_prompt, norm_gain, key_weight, value_weight, cache_keys, cache_values, resp_queries, resp_keys, resp_values, drift_ids, drift_count):
    gain = norm_gain.astype(jnp.float32)
    key_full = key_weight.astype(jnp.float32)
    value_full = value_weight.astype(jnp.float32)

    def shard(s, caches):

        def one(j, inner):
            block_id = drift_ids[s, j]
            start = (s * CTX_DEV + block_id * BLOCK).astype(jnp.int32)
            rows = lax.dynamic_slice_in_dim(x_prompt, start, BLOCK, 0)
            normed = lax.optimization_barrier(normalize(rows, gain)).astype(jnp.float32)
            fresh_k = jnp.dot(normed, key_full, precision=lax.Precision.HIGHEST).astype(jnp.bfloat16)
            fresh_v = jnp.dot(normed, value_full, precision=lax.Precision.HIGHEST).astype(jnp.bfloat16)
            return (lax.dynamic_update_slice_in_dim(inner[0], fresh_k, start, 0), lax.dynamic_update_slice_in_dim(inner[1], fresh_v, start, 0))
        return lax.fori_loop(jnp.int32(0), drift_count[s], one, caches)
    new_keys, new_values = lax.fori_loop(jnp.int32(0), jnp.int32(N_CTX), shard, (cache_keys, cache_values))
    scale = 1.0 / HD ** 0.5

    def per_head(head_index):
        start = (head_index * HD).astype(jnp.int32)
        query = lax.dynamic_slice_in_dim(resp_queries, start, HD, 1).astype(jnp.float32)
        pk = lax.dynamic_slice_in_dim(new_keys, start, HD, 1).astype(jnp.float32).reshape(N_CTX, CTX_DEV, HD)
        rk = lax.dynamic_slice_in_dim(resp_keys, start, HD, 1).astype(jnp.float32).reshape(N_CTX, RESP_DEV, HD)
        pv = lax.dynamic_slice_in_dim(new_values, start, HD, 1).astype(jnp.float32).reshape(N_CTX, CTX_DEV, HD)
        rv = lax.dynamic_slice_in_dim(resp_values, start, HD, 1).astype(jnp.float32).reshape(N_CTX, RESP_DEV, HD)
        keys = jnp.concatenate([pk, rk], axis=1)
        values = jnp.concatenate([pv, rv], axis=1)
        scores = jnp.einsum('rd,skd->rsk', query, keys, precision=lax.Precision.HIGHEST) * scale
        group_top = lax.optimization_barrier(jnp.max(scores, axis=2))
        top = lax.optimization_barrier(jnp.max(group_top, axis=1, keepdims=True))
        weights = jnp.exp(scores - group_top[:, :, None])
        factor = jnp.exp(group_top - top)
        rounded = lax.optimization_barrier(weights.astype(jnp.bfloat16)).astype(jnp.float32)
        partial_mix = jnp.einsum('rsk,skd->rsd', rounded, values, precision=lax.Precision.HIGHEST)
        mixed = lax.optimization_barrier(jnp.sum(partial_mix * factor[:, :, None], axis=1))
        total = lax.optimization_barrier(jnp.sum(lax.optimization_barrier(jnp.sum(weights, axis=2)) * factor, axis=1, keepdims=True))
        return mixed / total
    outputs = lax.map(per_head, jnp.arange(HEADS, dtype=jnp.int32))
    attended = jnp.transpose(outputs, (1, 0, 2)).reshape(RESP, HEADS * HD).astype(jnp.bfloat16)
    return (new_keys, new_values, attended)
```

```python
import jax
import jax.numpy as jnp
from jax import lax
from jax.experimental import pallas as pl
from jax.experimental.pallas import tpu as pltpu
from jax.sharding import PartitionSpec as P

HD = 128
BLOCK = 128
NY, NX, NZ = 8, 4, 8
WROWS = 64
eps = 1e-05
LOG2E = 1.4426950408889634
F32 = jnp.float32
BF16 = jnp.bfloat16


def shift_ctx(array, dy=0, dx=0, dcore=0):
    pairs = []
    for y in range(NY):
        for x in range(NX):
            for core in range(2):
                to = (((y + dy) % NY) * NX + (x + dx) % NX) * 2 + (core ^ dcore)
                pairs.append(((y * NX + x) * 2 + core, to))
    return lax.ppermute(array, "ctx", pairs)


def put_stats(stats, lane, h, top, total):
    for first, rest in ((h * 8, top), (h * 8 + 3, total)):
        for i in range(3):
            part = rest.astype(BF16).astype(F32)
            stats = jnp.where(lane == first + i, part, stats)
            rest = rest - part
    return stats


def get_stats(stats, h):
    one = [stats[..., h * 8 + i : h * 8 + i + 1] for i in range(6)]
    return one[0] + one[1] + one[2], one[3] + one[4] + one[5]


def column_kernel(pos, *refs):
    pieces, out, held = refs[:NY], refs[NY], refs[NY + 1]
    y = pos[0]
    for a, piece in enumerate(pieces):
        row = lax.rem(y + a, NY)
        out[row] = piece[:WROWS, :]
        out[NY + row] = piece[WROWS : 2 * WROWS, :]
        held[pl.ds(pl.multiple_of(row * 8, 8), 8), :] = piece[2 * WROWS :, :].astype(F32)
    out[2 * NY] = held[...].astype(BF16)


def payload_kernel(keys, values, queries, out):
    out[:WROWS, :] = keys[...]
    out[WROWS : 2 * WROWS, :] = values[...]
    out[2 * WROWS :, :] = queries[...]


def place_from(pos):
    x, core = pos[1], pos[2]
    return lambda b, e: lax.rem(x + b, NX) * 2 + (core + e - 2 * core * e)


def project_kernel(pos, gain, xs, own, own_sw, following, last, turned, acc, pair):
    slices, rows, depth = xs.shape
    width = own.shape[2]
    pair[0] = following[...]
    pair[1] = last[...]

    def squares(j, total):
        part = xs[j].astype(F32)
        part = part * part
        return total + sum(part[:, i * 128 : (i + 1) * 128] for i in range(part.shape[1] // 128))

    summed = lax.fori_loop(0, slices, squares, jnp.zeros((rows, 128), F32))
    mean = jnp.sum(summed, axis=1, keepdims=True) * (1.0 / (slices * depth))
    scale = lax.rsqrt(mean + eps)
    low = lax.broadcasted_iota(jnp.int32, (rows, 128), 1) < WROWS
    for q in range(NX):
        cols = slice(q * 128, (q + 1) * 128)
        for u in range(slices // 2):
            one, two = (xs[j, :, cols].astype(F32) * scale * gain[j : j + 1, cols] for j in (2 * u, 2 * u + 1))
            at = slice(u * 128, (u + 1) * 128)
            turned[2 * q, :, at] = jnp.where(low, one, pltpu.roll(two, WROWS, 1)).astype(BF16)
            turned[2 * q + 1, :, at] = jnp.where(low, pltpu.roll(one, WROWS, 1), two).astype(BF16)
    place = place_from(pos)
    acc[...] = jnp.zeros_like(acc)
    for piece, b, e in ((own, 0, 0), (own_sw, 0, 1), (following, 1, 0), (last, 3, 0)):
        left = turned[place(b, e)]
        acc[:, :width] += jnp.dot(left, piece[:NY].reshape(depth, width), preferred_element_type=F32)
        acc[:, width:] += jnp.dot(left, piece[NY : 2 * NY].reshape(depth, width), preferred_element_type=F32)


def fused_kernel(*refs):
    pos, cache_k, cache_v, resp_k, resp_v, normed, acc_in = refs[:7]
    own, own_sw, pair, pair_sw, far_k, far_k_sw, far_v, far_v_sw = refs[7:15]
    new_k, new_v, packed_mine, packed_other, queries, keys, values, acc = refs[15:]
    rows, depth = normed.shape[1:]
    width = own.shape[2]
    x = pos[1]
    place = place_from(pos)

    for e, (mine, two, far) in enumerate(((own, pair, far_v), (own_sw, pair_sw, far_v_sw))):
        for b, block in enumerate((mine[2 * NY], two[0, 2 * NY], far[NY], two[1, 2 * NY])):
            queries[e * NX + lax.rem(x + b, NX)] = block
    acc[...] = acc_in[...]
    for left, of_k, of_v in (
        (place(1, 1), pair_sw[0, :NY], pair_sw[0, NY : 2 * NY]),
        (place(3, 1), pair_sw[1, :NY], pair_sw[1, NY : 2 * NY]),
        (place(2, 0), far_k[...], far_v[:NY]),
        (place(2, 1), far_k_sw[...], far_v_sw[:NY]),
    ):
        acc[:, :width] += jnp.dot(normed[left], of_k.reshape(depth, width), preferred_element_type=F32)
        acc[:, width:] += jnp.dot(normed[left], of_v.reshape(depth, width), preferred_element_type=F32)

    for b in range(rows // BLOCK):
        at = slice(b * BLOCK, (b + 1) * BLOCK)
        drifted = pos[4 + b] > 0
        keys[at, :] = jnp.where(drifted, acc[at, :width].astype(BF16), cache_k[at, :])
        values[at, :] = jnp.where(drifted, acc[at, width:].astype(BF16), cache_v[at, :])
    new_k[...] = keys[:rows, :]
    new_v[...] = values[:rows, :]
    blank = jnp.zeros((128 - resp_k.shape[0], width), F32)
    keys[rows:, :] = jnp.concatenate([resp_k[...].astype(F32), blank], axis=0).astype(BF16)
    values[rows:, :] = jnp.concatenate([resp_v[...].astype(F32), blank], axis=0).astype(BF16)
    tile = packed_mine.shape[0]
    lane = lax.broadcasted_iota(jnp.int32, (tile, 128), 1)
    score_scale = 1.0 / HD**0.5
    for t, packed in enumerate((packed_mine, packed_other)):
        query = queries[t * NX : (t + 1) * NX].reshape(tile, width)
        stats = jnp.zeros((tile, 128), F32)
        for h in range(width // HD):
            cols = slice(h * HD, (h + 1) * HD)
            scores = lax.dot_general(
                query[:, cols], keys[:, cols], (((1,), (1,)), ((), ())), preferred_element_type=F32
            )
            extra = jnp.where(lane < 8, scores[:, rows:], -jnp.inf)
            scores = scores[:, :rows]
            top = jnp.maximum(jnp.max(scores, axis=1, keepdims=True), jnp.max(extra, axis=1, keepdims=True))
            weights = jnp.exp2((scores - top) * (LOG2E * score_scale))
            extra = jnp.exp2((extra - top) * (LOG2E * score_scale))
            total = jnp.sum(weights, axis=1, keepdims=True) + jnp.sum(extra, axis=1, keepdims=True)
            weights = jnp.concatenate([weights.astype(BF16), extra.astype(BF16)], axis=1)
            packed[:, cols] = jnp.dot(weights, values[:, cols], preferred_element_type=F32).astype(BF16)
            stats = put_stats(stats, lane, h, top * score_scale, total)
        packed[:, width:] = stats.astype(BF16)


def merge_kernel(one, two, out):
    width = out.shape[1] - 128
    lane = lax.broadcasted_iota(jnp.int32, (out.shape[0], 128), 1)
    stats = [ref[:, width:].astype(F32) for ref in (one, two)]
    merged = jnp.zeros(lane.shape, F32)
    for h in range(width // HD):
        cols = slice(h * HD, (h + 1) * HD)
        (top_one, total_one), (top_two, total_two) = (get_stats(s, h) for s in stats)
        top = jnp.maximum(top_one, top_two)
        factor_one, factor_two = jnp.exp(top_one - top), jnp.exp(top_two - top)
        out[:, cols] = (one[:, cols].astype(F32) * factor_one + two[:, cols].astype(F32) * factor_two).astype(BF16)
        merged = put_stats(merged, lane, h, top, total_one * factor_one + total_two * factor_two)
    out[:, width:] = merged.astype(BF16)


def combine_kernel(parts, out):
    groups, rows = parts.shape[0] // 8, 8
    width = out.shape[1]
    stats = parts[:, width:].astype(F32).reshape(groups, rows, 128)
    for h in range(width // HD):
        cols = slice(h * HD, (h + 1) * HD)
        top, total = get_stats(stats, h)
        factor = jnp.exp(top - jnp.max(top, axis=0, keepdims=True))
        mix = parts[:, cols].astype(F32).reshape(groups, rows, HD)
        mixed = jnp.sum(mix * factor, axis=0)
        out[:, cols] = (mixed / jnp.sum(total * factor, axis=0)).astype(BF16)


def body(
    x_prompt,
    norm_gain,
    key_weight,
    value_weight,
    cache_keys,
    cache_values,
    resp_queries,
    resp_keys,
    resp_values,
    drift_ids,
    drift_count,
):
    here = lax.axis_index("ctx")
    z = lax.axis_index("head")
    y, x, core = here // (NX * 2), (here // 2) % NX, here % 2
    rows, slice_width = x_prompt.shape
    width = key_weight.shape[1]
    mine_ids = lax.dynamic_index_in_dim(drift_ids, here, 0, keepdims=False)
    count_me = lax.dynamic_index_in_dim(drift_count, here, 0, keepdims=False)
    slots = jnp.arange(drift_ids.shape[1])
    drifted = jnp.any((mine_ids[None, :] == slots[:, None]) & (slots < count_me)[None, :], axis=1)
    pos = jnp.concatenate([jnp.stack([y, x, core, z]).astype(jnp.int32), drifted.astype(jnp.int32)])

    vmem = pl.BlockSpec(memory_space=pltpu.VMEM)
    smem = pl.BlockSpec(memory_space=pltpu.SMEM)
    big = pltpu.CompilerParams(vmem_limit_bytes=30 << 20)
    x_all = lax.all_gather(x_prompt, "head", axis=0)

    payload = pl.pallas_call(
        payload_kernel,
        out_shape=jax.ShapeDtypeStruct((2 * WROWS + resp_queries.shape[0], width), BF16),
        in_specs=[vmem] * 3,
        out_specs=vmem,
        compiler_params=pltpu.CompilerParams(vmem_limit_bytes=16 << 20),
        name="payload",
    )(key_weight, value_weight, resp_queries)
    near = {a: shift_ctx(payload, dy=-a) for a in (3, 5, 2, 6, 1, 7)}
    near[4] = shift_ctx(near[5], dy=1)
    column = pl.pallas_call(
        column_kernel,
        out_shape=jax.ShapeDtypeStruct((2 * NY + 1, WROWS, width), BF16),
        in_specs=[smem] + [vmem] * NY,
        out_specs=vmem,
        scratch_shapes=[pltpu.VMEM((NY * resp_queries.shape[0], width), F32)],
        compiler_params=pltpu.CompilerParams(vmem_limit_bytes=16 << 20),
        name="column",
    )(pos, payload, *[near[a] for a in range(1, NY)])
    following, last = shift_ctx(column, dx=-1), shift_ctx(column, dx=1)
    far_k, far_v = shift_ctx(last[:NY], dx=1), shift_ctx(following[NY:], dx=-1)
    own_sw = shift_ctx(column, dcore=1)
    normed, partial, pair = pl.pallas_call(
        project_kernel,
        out_shape=(
            jax.ShapeDtypeStruct((NZ, rows, slice_width), BF16),
            jax.ShapeDtypeStruct((rows, 2 * width), F32),
            jax.ShapeDtypeStruct((2,) + column.shape, BF16),
        ),
        in_specs=[smem] + [vmem] * 6,
        out_specs=(vmem, vmem, vmem),
        compiler_params=big,
        cost_estimate=pl.CostEstimate(flops=3 << 30, bytes_accessed=24 << 20, transcendentals=512),
        name="norm_project",
    )(pos, norm_gain.astype(F32).reshape(NZ, slice_width), x_all, column, own_sw, following, last)
    pair_sw = shift_ctx(lax.optimization_barrier((pair, far_k, far_v))[0], dcore=1)
    far_k_sw, far_v_sw = shift_ctx(far_k, dcore=1), shift_ctx(far_v, dcore=1)

    total = 2 * NY * NX * resp_queries.shape[0]
    result = jax.ShapeDtypeStruct((total // 2, width + 128), BF16)
    new_keys, new_values, packed_mine, packed_other = pl.pallas_call(
        fused_kernel,
        out_shape=(
            jax.ShapeDtypeStruct((rows, width), BF16),
            jax.ShapeDtypeStruct((rows, width), BF16),
            result,
            result,
        ),
        in_specs=[smem] + [vmem] * 14,
        out_specs=(vmem, vmem, vmem, vmem),
        scratch_shapes=[
            pltpu.VMEM((2 * NX, WROWS, width), BF16),
            pltpu.VMEM((rows + 128, width), BF16),
            pltpu.VMEM((rows + 128, width), BF16),
            pltpu.VMEM((rows, 2 * width), F32),
        ],
        compiler_params=big,
        cost_estimate=pl.CostEstimate(flops=3 << 30, bytes_accessed=12 << 20, transcendentals=1 << 20),
        name="refresh_attend",
    )(
        pos,
        cache_keys,
        cache_values,
        resp_keys,
        resp_values,
        normed,
        partial,
        column,
        own_sw,
        pair,
        pair_sw,
        far_k,
        far_k_sw,
        far_v,
        far_v_sw,
    )
    merged = pl.pallas_call(
        merge_kernel,
        out_shape=result,
        in_specs=[vmem, vmem],
        out_specs=vmem,
        compiler_params=pltpu.CompilerParams(vmem_limit_bytes=16 << 20),
        name="merge",
    )(packed_mine, shift_ctx(packed_other, dcore=1))
    same = [[(j * NX + i) * 2 + c for i in range(NX) for j in range(NY)] for c in range(2)]
    parts = lax.all_to_all(merged, "ctx", 0, 0, axis_index_groups=same, tiled=True)
    attended = pl.pallas_call(
        combine_kernel,
        out_shape=jax.ShapeDtypeStruct((resp_queries.shape[0], width), BF16),
        in_specs=[vmem],
        out_specs=vmem,
        compiler_params=pltpu.CompilerParams(vmem_limit_bytes=16 << 20),
        name="combine",
    )(parts)
    return new_keys, new_values, attended


def solution(mesh):
    placed = (
        P("ctx", "head"),
        P(),
        P("ctx", "head"),
        P("ctx", "head"),
        P("ctx", "head"),
        P("ctx", "head"),
        P("ctx", "head"),
        P("ctx", "head"),
        P("ctx", "head"),
        P(),
        P(),
    )
    return jax.shard_map(
        body,
        mesh=mesh,
        in_specs=placed,
        out_specs=(P("ctx", "head"), P("ctx", "head"), P("ctx", "head")),
        check_vma=False,
    )
```

```python
import jax
import jax.numpy as jnp
from jax import lax
from jax.experimental import pallas as pl
from jax.experimental.pallas import tpu as pltpu
from jax.sharding import PartitionSpec as P

HD = 128
BLOCK = 128
NY, NX, NZ = 8, 4, 8
WROWS = 64
eps = 1e-05
LOG2E = 1.4426950408889634
F32 = jnp.float32
BF16 = jnp.bfloat16


def shift_ctx(array, dy=0, dx=0, dcore=0):
    pairs = []
    for y in range(NY):
        for x in range(NX):
            for core in range(2):
                to = (((y + dy) % NY) * NX + (x + dx) % NX) * 2 + (core ^ dcore)
                pairs.append(((y * NX + x) * 2 + core, to))
    return lax.ppermute(array, "ctx", pairs)


def put_stats(stats, lane, h, top, total):
    for first, rest in ((h * 8, top), (h * 8 + 3, total)):
        for i in range(3):
            part = rest.astype(BF16).astype(F32)
            stats = jnp.where(lane == first + i, part, stats)
            rest = rest - part
    return stats


def get_stats(stats, h):
    one = [stats[..., h * 8 + i : h * 8 + i + 1] for i in range(6)]
    return one[0] + one[1] + one[2], one[3] + one[4] + one[5]


def column_kernel(pos, *refs):
    pieces, out, held = refs[:NY], refs[NY], refs[NY + 1]
    y = pos[0]
    for a, piece in enumerate(pieces):
        row = lax.rem(y + a, NY)
        out[row] = piece[:WROWS, :]
        out[NY + row] = piece[WROWS : 2 * WROWS, :]
        held[pl.ds(pl.multiple_of(row * 8, 8), 8), :] = piece[2 * WROWS :, :].astype(F32)
    out[2 * NY] = held[...].astype(BF16)


def payload_kernel(keys, values, queries, out):
    out[:WROWS, :] = keys[...]
    out[WROWS : 2 * WROWS, :] = values[...]
    out[2 * WROWS :, :] = queries[...]


def place_from(pos):
    x, core = pos[1], pos[2]
    return lambda b, e: lax.rem(x + b, NX) * 2 + (core + e - 2 * core * e)


def project_kernel(pos, gain, xs, own, own_sw, following, last, turned, acc, pair):
    slices, rows, depth = xs.shape
    width = own.shape[2]
    pair[0] = following[...]
    pair[1] = last[...]

    def squares(j, total):
        part = xs[j].astype(F32)
        part = part * part
        return total + sum(part[:, i * 128 : (i + 1) * 128] for i in range(part.shape[1] // 128))

    summed = lax.fori_loop(0, slices, squares, jnp.zeros((rows, 128), F32))
    mean = jnp.sum(summed, axis=1, keepdims=True) * (1.0 / (slices * depth))
    scale = lax.rsqrt(mean + eps)
    low = lax.broadcasted_iota(jnp.int32, (rows, 128), 1) < WROWS
    for q in range(NX):
        cols = slice(q * 128, (q + 1) * 128)
        for u in range(slices // 2):
            one, two = (xs[j, :, cols].astype(F32) * scale * gain[j : j + 1, cols] for j in (2 * u, 2 * u + 1))
            at = slice(u * 128, (u + 1) * 128)
            turned[2 * q, :, at] = jnp.where(low, one, pltpu.roll(two, WROWS, 1)).astype(BF16)
            turned[2 * q + 1, :, at] = jnp.where(low, pltpu.roll(one, WROWS, 1), two).astype(BF16)
    place = place_from(pos)
    acc[...] = jnp.zeros_like(acc)
    for piece, b, e in ((own, 0, 0), (own_sw, 0, 1), (following, 1, 0), (last, 3, 0)):
        left = turned[place(b, e)]
        acc[:, :width] += jnp.dot(left, piece[:NY].reshape(depth, width), preferred_element_type=F32)
        acc[:, width:] += jnp.dot(left, piece[NY : 2 * NY].reshape(depth, width), preferred_element_type=F32)


def fused_kernel(*refs):
    pos, cache_k, cache_v, resp_k, resp_v, normed, acc_in = refs[:7]
    own, own_sw, pair, pair_sw, far_k, far_k_sw, far_v, far_v_sw = refs[7:15]
    new_k, new_v, packed_mine, packed_other, queries, keys, values, acc = refs[15:]
    rows, depth = normed.shape[1:]
    width = own.shape[2]
    x = pos[1]
    place = place_from(pos)

    for e, (mine, two, far) in enumerate(((own, pair, far_v), (own_sw, pair_sw, far_v_sw))):
        for b, block in enumerate((mine[2 * NY], two[0, 2 * NY], far[NY], two[1, 2 * NY])):
            queries[e * NX + lax.rem(x + b, NX)] = block
    acc[...] = acc_in[...]
    for left, of_k, of_v in (
        (place(1, 1), pair_sw[0, :NY], pair_sw[0, NY : 2 * NY]),
        (place(3, 1), pair_sw[1, :NY], pair_sw[1, NY : 2 * NY]),
        (place(2, 0), far_k[...], far_v[:NY]),
        (place(2, 1), far_k_sw[...], far_v_sw[:NY]),
    ):
        acc[:, :width] += jnp.dot(normed[left], of_k.reshape(depth, width), preferred_element_type=F32)
        acc[:, width:] += jnp.dot(normed[left], of_v.reshape(depth, width), preferred_element_type=F32)

    for b in range(rows // BLOCK):
        at = slice(b * BLOCK, (b + 1) * BLOCK)
        drifted = pos[4 + b] > 0
        keys[at, :] = jnp.where(drifted, acc[at, :width].astype(BF16), cache_k[at, :])
        values[at, :] = jnp.where(drifted, acc[at, width:].astype(BF16), cache_v[at, :])
    new_k[...] = keys[:rows, :]
    new_v[...] = values[:rows, :]
    blank = jnp.zeros((128 - resp_k.shape[0], width), F32)
    keys[rows:, :] = jnp.concatenate([resp_k[...].astype(F32), blank], axis=0).astype(BF16)
    values[rows:, :] = jnp.concatenate([resp_v[...].astype(F32), blank], axis=0).astype(BF16)
    tile = packed_mine.shape[0]
    lane = lax.broadcasted_iota(jnp.int32, (tile, 128), 1)
    score_scale = 1.0 / HD**0.5
    for t, packed in enumerate((packed_mine, packed_other)):
        query = queries[t * NX : (t + 1) * NX].reshape(tile, width)
        stats = jnp.zeros((tile, 128), F32)
        for h in range(width // HD):
            cols = slice(h * HD, (h + 1) * HD)
            scores = lax.dot_general(
                query[:, cols], keys[:, cols], (((1,), (1,)), ((), ())), preferred_element_type=F32
            )
            extra = jnp.where(lane < 8, scores[:, rows:], -jnp.inf)
            scores = scores[:, :rows]
            top = jnp.maximum(jnp.max(scores, axis=1, keepdims=True), jnp.max(extra, axis=1, keepdims=True))
            weights = jnp.exp2((scores - top) * (LOG2E * score_scale))
            extra = jnp.exp2((extra - top) * (LOG2E * score_scale))
            total = jnp.sum(weights, axis=1, keepdims=True) + jnp.sum(extra, axis=1, keepdims=True)
            weights = jnp.concatenate([weights.astype(BF16), extra.astype(BF16)], axis=1)
            packed[:, cols] = jnp.dot(weights, values[:, cols], preferred_element_type=F32).astype(BF16)
            stats = put_stats(stats, lane, h, top * score_scale, total)
        packed[:, width:] = stats.astype(BF16)


def merge_kernel(one, two, out):
    width = out.shape[1] - 128
    lane = lax.broadcasted_iota(jnp.int32, (out.shape[0], 128), 1)
    stats = [ref[:, width:].astype(F32) for ref in (one, two)]
    merged = jnp.zeros(lane.shape, F32)
    for h in range(width // HD):
        cols = slice(h * HD, (h + 1) * HD)
        (top_one, total_one), (top_two, total_two) = (get_stats(s, h) for s in stats)
        top = jnp.maximum(top_one, top_two)
        factor_one, factor_two = jnp.exp(top_one - top), jnp.exp(top_two - top)
        out[:, cols] = (one[:, cols].astype(F32) * factor_one + two[:, cols].astype(F32) * factor_two).astype(BF16)
        merged = put_stats(merged, lane, h, top, total_one * factor_one + total_two * factor_two)
    out[:, width:] = merged.astype(BF16)


def combine_kernel(parts, out):
    groups, rows = parts.shape[0] // 8, 8
    width = out.shape[1]
    stats = parts[:, width:].astype(F32).reshape(groups, rows, 128)
    for h in range(width // HD):
        cols = slice(h * HD, (h + 1) * HD)
        top, total = get_stats(stats, h)
        factor = jnp.exp(top - jnp.max(top, axis=0, keepdims=True))
        mix = parts[:, cols].astype(F32).reshape(groups, rows, HD)
        mixed = jnp.sum(mix * factor, axis=0)
        out[:, cols] = (mixed / jnp.sum(total * factor, axis=0)).astype(BF16)


def body(
    x_prompt,
    norm_gain,
    key_weight,
    value_weight,
    cache_keys,
    cache_values,
    resp_queries,
    resp_keys,
    resp_values,
    drift_ids,
    drift_count,
):
    here = lax.axis_index("ctx")
    z = lax.axis_index("head")
    y, x, core = here // (NX * 2), (here // 2) % NX, here % 2
    rows, slice_width = x_prompt.shape
    width = key_weight.shape[1]
    mine_ids = lax.dynamic_index_in_dim(drift_ids, here, 0, keepdims=False)
    count_me = lax.dynamic_index_in_dim(drift_count, here, 0, keepdims=False)
    slots = jnp.arange(drift_ids.shape[1])
    drifted = jnp.any((mine_ids[None, :] == slots[:, None]) & (slots < count_me)[None, :], axis=1)
    pos = jnp.concatenate([jnp.stack([y, x, core, z]).astype(jnp.int32), drifted.astype(jnp.int32)])

    vmem = pl.BlockSpec(memory_space=pltpu.VMEM)
    smem = pl.BlockSpec(memory_space=pltpu.SMEM)
    big = pltpu.CompilerParams(vmem_limit_bytes=16 << 20)
    x_all = lax.all_gather(x_prompt, "head", axis=0)

    payload = pl.pallas_call(
        payload_kernel,
        out_shape=jax.ShapeDtypeStruct((2 * WROWS + resp_queries.shape[0], width), BF16),
        in_specs=[vmem] * 3,
        out_specs=vmem,
        compiler_params=pltpu.CompilerParams(vmem_limit_bytes=16 << 20),
        name="payload",
    )(key_weight, value_weight, resp_queries)
    near = {a: shift_ctx(payload, dy=-a) for a in (3, 5, 2, 6, 1, 7)}
    near[4] = shift_ctx(near[5], dy=1)
    column = pl.pallas_call(
        column_kernel,
        out_shape=jax.ShapeDtypeStruct((2 * NY + 1, WROWS, width), BF16),
        in_specs=[smem] + [vmem] * NY,
        out_specs=vmem,
        scratch_shapes=[pltpu.VMEM((NY * resp_queries.shape[0], width), F32)],
        compiler_params=pltpu.CompilerParams(vmem_limit_bytes=16 << 20),
        name="column",
    )(pos, payload, *[near[a] for a in range(1, NY)])
    following, last = shift_ctx(column, dx=-1), shift_ctx(column, dx=1)
    far_k, far_v = shift_ctx(last[:NY], dx=1), shift_ctx(following[NY:], dx=-1)
    own_sw = shift_ctx(column, dcore=1)
    normed, partial, pair = pl.pallas_call(
        project_kernel,
        out_shape=(
            jax.ShapeDtypeStruct((NZ, rows, slice_width), BF16),
            jax.ShapeDtypeStruct((rows, 2 * width), F32),
            jax.ShapeDtypeStruct((2,) + column.shape, BF16),
        ),
        in_specs=[smem] + [vmem] * 6,
        out_specs=(vmem, vmem, vmem),
        compiler_params=big,
        cost_estimate=pl.CostEstimate(flops=3 << 30, bytes_accessed=24 << 20, transcendentals=512),
        name="norm_project",
    )(pos, norm_gain.astype(F32).reshape(NZ, slice_width), x_all, column, own_sw, following, last)
    pair_sw = shift_ctx(lax.optimization_barrier((pair, far_k, far_v))[0], dcore=1)
    far_k_sw, far_v_sw = shift_ctx(far_k, dcore=1), shift_ctx(far_v, dcore=1)

    total = 2 * NY * NX * resp_queries.shape[0]
    result = jax.ShapeDtypeStruct((total // 2, width + 128), BF16)
    new_keys, new_values, packed_mine, packed_other = pl.pallas_call(
        fused_kernel,
        out_shape=(
            jax.ShapeDtypeStruct((rows, width), BF16),
            jax.ShapeDtypeStruct((rows, width), BF16),
            result,
            result,
        ),
        in_specs=[smem] + [vmem] * 14,
        out_specs=(vmem, vmem, vmem, vmem),
        scratch_shapes=[
            pltpu.VMEM((2 * NX, WROWS, width), BF16),
            pltpu.VMEM((rows + 128, width), BF16),
            pltpu.VMEM((rows + 128, width), BF16),
            pltpu.VMEM((rows, 2 * width), F32),
        ],
        compiler_params=big,
        cost_estimate=pl.CostEstimate(flops=3 << 30, bytes_accessed=12 << 20, transcendentals=1 << 20),
        name="refresh_attend",
    )(
        pos,
        cache_keys,
        cache_values,
        resp_keys,
        resp_values,
        normed,
        partial,
        column,
        own_sw,
        pair,
        pair_sw,
        far_k,
        far_k_sw,
        far_v,
        far_v_sw,
    )
    merged = pl.pallas_call(
        merge_kernel,
        out_shape=result,
        in_specs=[vmem, vmem],
        out_specs=vmem,
        compiler_params=pltpu.CompilerParams(vmem_limit_bytes=16 << 20),
        name="merge",
    )(packed_mine, shift_ctx(packed_other, dcore=1))
    same = [[(j * NX + i) * 2 + c for i in range(NX) for j in range(NY)] for c in range(2)]
    parts = lax.all_to_all(merged, "ctx", 0, 0, axis_index_groups=same, tiled=True)
    attended = pl.pallas_call(
        combine_kernel,
        out_shape=jax.ShapeDtypeStruct((resp_queries.shape[0], width), BF16),
        in_specs=[vmem],
        out_specs=vmem,
        compiler_params=pltpu.CompilerParams(vmem_limit_bytes=16 << 20),
        name="combine",
    )(parts)
    return new_keys, new_values, attended


def solution(mesh):
    placed = (
        P("ctx", "head"),
        P(),
        P("ctx", "head"),
        P("ctx", "head"),
        P("ctx", "head"),
        P("ctx", "head"),
        P("ctx", "head"),
        P("ctx", "head"),
        P("ctx", "head"),
        P(),
        P(),
    )
    return jax.shard_map(
        body,
        mesh=mesh,
        in_specs=placed,
        out_specs=(P("ctx", "head"), P("ctx", "head"), P("ctx", "head")),
        check_vma=False,
    )
```

```python
import jax
import jax.numpy as jnp
from jax import lax
from jax.experimental import pallas as pl
from jax.experimental.pallas import tpu as pltpu
from jax.sharding import PartitionSpec as P

HD = 128
BLOCK = 128
NY, NX, NZ = 8, 4, 8
WROWS = 64
eps = 1e-05
LOG2E = 1.4426950408889634
F32 = jnp.float32
BF16 = jnp.bfloat16


def shift_ctx(array, dy=0, dx=0, dcore=0):
    pairs = []
    for y in range(NY):
        for x in range(NX):
            for core in range(2):
                to = (((y + dy) % NY) * NX + (x + dx) % NX) * 2 + (core ^ dcore)
                pairs.append(((y * NX + x) * 2 + core, to))
    return lax.ppermute(array, "ctx", pairs)


def put_stats(stats, lane, h, top, total):
    for first, rest in ((h * 8, top), (h * 8 + 3, total)):
        for i in range(3):
            part = rest.astype(BF16).astype(F32)
            stats = jnp.where(lane == first + i, part, stats)
            rest = rest - part
    return stats


def get_stats(stats, h):
    one = [stats[..., h * 8 + i : h * 8 + i + 1] for i in range(6)]
    return one[0] + one[1] + one[2], one[3] + one[4] + one[5]


def column_kernel(pos, *refs):
    pieces, gain, out, gain_out, held = refs[:NY], *refs[NY:]
    gain_out[...] = gain[...]
    y = pos[0]
    for a, piece in enumerate(pieces):
        row = lax.rem(y + a, NY)
        out[row] = piece[:WROWS, :]
        out[NY + row] = piece[WROWS : 2 * WROWS, :]
        held[pl.ds(pl.multiple_of(row * 8, 8), 8), :] = piece[2 * WROWS :, :].astype(F32)
    out[2 * NY] = held[...].astype(BF16)


def part_kernel(first, piece, out):
    out[...] = piece[first : first + out.shape[0]]


def join_kernel(one, two, out):
    out[: one.shape[0]] = one[...]
    out[one.shape[0] :] = two[...]


def payload_kernel(keys, values, queries, out):
    out[:WROWS, :] = keys[...]
    out[WROWS : 2 * WROWS, :] = values[...]
    out[2 * WROWS :, :] = queries[...]


def place_from(pos):
    x, core = pos[1], pos[2]
    return lambda b, e: lax.rem(x + b, NX) * 2 + (core + e - 2 * core * e)


def project_kernel(pos, gain, xs, own, own_sw, following, last, turned, acc, pair):
    slices, rows, depth = xs.shape
    width = own.shape[2]
    pair[0] = following[...]
    pair[1] = last[...]

    def squares(j, total):
        part = xs[j].astype(F32)
        part = part * part
        return total + sum(part[:, i * 128 : (i + 1) * 128] for i in range(part.shape[1] // 128))

    summed = lax.fori_loop(0, slices, squares, jnp.zeros((rows, 128), F32))
    mean = jnp.sum(summed, axis=1, keepdims=True) * (1.0 / (slices * depth))
    scale = lax.rsqrt(mean + eps)
    low = lax.broadcasted_iota(jnp.int32, (rows, 128), 1) < WROWS
    for q in range(NX):
        cols = slice(q * 128, (q + 1) * 128)
        for u in range(slices // 2):
            one, two = (xs[j, :, cols].astype(F32) * scale * gain[j : j + 1, cols] for j in (2 * u, 2 * u + 1))
            at = slice(u * 128, (u + 1) * 128)
            turned[2 * q, :, at] = jnp.where(low, one, pltpu.roll(two, WROWS, 1)).astype(BF16)
            turned[2 * q + 1, :, at] = jnp.where(low, pltpu.roll(one, WROWS, 1), two).astype(BF16)
    place = place_from(pos)
    acc[...] = jnp.zeros_like(acc)
    for piece, b, e in ((own, 0, 0), (own_sw, 0, 1), (following, 1, 0), (last, 3, 0)):
        left = turned[place(b, e)]
        acc[:, :width] += jnp.dot(left, piece[:NY].reshape(depth, width), preferred_element_type=F32)
        acc[:, width:] += jnp.dot(left, piece[NY : 2 * NY].reshape(depth, width), preferred_element_type=F32)


def fused_kernel(*refs):
    pos, cache_k, cache_v, resp_k, resp_v, normed, acc_in = refs[:7]
    own, own_sw, pair, pair_sw, far, far_sw = refs[7:13]
    new_k, new_v, packed_mine, packed_other, queries, keys, values, acc = refs[13:]
    rows, depth = normed.shape[1:]
    width = own.shape[2]
    x = pos[1]
    place = place_from(pos)

    for e, (mine, two, third) in enumerate(((own, pair, far), (own_sw, pair_sw, far_sw))):
        for b, block in enumerate((mine[2 * NY], two[0, 2 * NY], third[2 * NY], two[1, 2 * NY])):
            queries[e * NX + lax.rem(x + b, NX)] = block
    acc[...] = acc_in[...]
    for left, of_k, of_v in (
        (place(1, 1), pair_sw[0, :NY], pair_sw[0, NY : 2 * NY]),
        (place(3, 1), pair_sw[1, :NY], pair_sw[1, NY : 2 * NY]),
        (place(2, 0), far[:NY], far[NY : 2 * NY]),
        (place(2, 1), far_sw[:NY], far_sw[NY : 2 * NY]),
    ):
        acc[:, :width] += jnp.dot(normed[left], of_k.reshape(depth, width), preferred_element_type=F32)
        acc[:, width:] += jnp.dot(normed[left], of_v.reshape(depth, width), preferred_element_type=F32)

    for b in range(rows // BLOCK):
        at = slice(b * BLOCK, (b + 1) * BLOCK)
        drifted = pos[4 + b] > 0
        keys[at, :] = jnp.where(drifted, acc[at, :width].astype(BF16), cache_k[at, :])
        values[at, :] = jnp.where(drifted, acc[at, width:].astype(BF16), cache_v[at, :])
    new_k[...] = keys[:rows, :]
    new_v[...] = values[:rows, :]
    blank = jnp.zeros((128 - resp_k.shape[0], width), F32)
    keys[rows:, :] = jnp.concatenate([resp_k[...].astype(F32), blank], axis=0).astype(BF16)
    values[rows:, :] = jnp.concatenate([resp_v[...].astype(F32), blank], axis=0).astype(BF16)
    tile = packed_mine.shape[0]
    lane = lax.broadcasted_iota(jnp.int32, (tile, 128), 1)
    score_scale = 1.0 / HD**0.5
    for t, packed in enumerate((packed_mine, packed_other)):
        query = queries[t * NX : (t + 1) * NX].reshape(tile, width)
        stats = jnp.zeros((tile, 128), F32)
        for h in range(width // HD):
            cols = slice(h * HD, (h + 1) * HD)
            scores = lax.dot_general(
                query[:, cols], keys[:, cols], (((1,), (1,)), ((), ())), preferred_element_type=F32
            )
            extra = jnp.where(lane < 8, scores[:, rows:], -jnp.inf)
            scores = scores[:, :rows]
            top = jnp.maximum(jnp.max(scores, axis=1, keepdims=True), jnp.max(extra, axis=1, keepdims=True))
            weights = jnp.exp2((scores - top) * (LOG2E * score_scale))
            extra = jnp.exp2((extra - top) * (LOG2E * score_scale))
            total = jnp.sum(weights, axis=1, keepdims=True) + jnp.sum(extra, axis=1, keepdims=True)
            weights = jnp.concatenate([weights.astype(BF16), extra.astype(BF16)], axis=1)
            packed[:, cols] = jnp.dot(weights, values[:, cols], preferred_element_type=F32).astype(BF16)
            stats = put_stats(stats, lane, h, top * score_scale, total)
        packed[:, width:] = stats.astype(BF16)


def merge_kernel(one, two, out):
    width = out.shape[1] - 128
    lane = lax.broadcasted_iota(jnp.int32, (out.shape[0], 128), 1)
    stats = [ref[:, width:].astype(F32) for ref in (one, two)]
    merged = jnp.zeros(lane.shape, F32)
    for h in range(width // HD):
        cols = slice(h * HD, (h + 1) * HD)
        (top_one, total_one), (top_two, total_two) = (get_stats(s, h) for s in stats)
        top = jnp.maximum(top_one, top_two)
        factor_one, factor_two = jnp.exp(top_one - top), jnp.exp(top_two - top)
        out[:, cols] = (one[:, cols].astype(F32) * factor_one + two[:, cols].astype(F32) * factor_two).astype(BF16)
        merged = put_stats(merged, lane, h, top, total_one * factor_one + total_two * factor_two)
    out[:, width:] = merged.astype(BF16)


def combine_kernel(parts, out):
    groups, rows = parts.shape[0] // 8, 8
    width = out.shape[1]
    stats = parts[:, width:].astype(F32).reshape(groups, rows, 128)
    for h in range(width // HD):
        cols = slice(h * HD, (h + 1) * HD)
        top, total = get_stats(stats, h)
        factor = jnp.exp(top - jnp.max(top, axis=0, keepdims=True))
        mix = parts[:, cols].astype(F32).reshape(groups, rows, HD)
        mixed = jnp.sum(mix * factor, axis=0)
        out[:, cols] = (mixed / jnp.sum(total * factor, axis=0)).astype(BF16)


def body(
    x_prompt,
    norm_gain,
    key_weight,
    value_weight,
    cache_keys,
    cache_values,
    resp_queries,
    resp_keys,
    resp_values,
    drift_ids,
    drift_count,
):
    here = lax.axis_index("ctx")
    z = lax.axis_index("head")
    y, x, core = here // (NX * 2), (here // 2) % NX, here % 2
    rows, slice_width = x_prompt.shape
    width = key_weight.shape[1]
    mine_ids = lax.dynamic_index_in_dim(drift_ids, here, 0, keepdims=False)
    count_me = lax.dynamic_index_in_dim(drift_count, here, 0, keepdims=False)
    slots = jnp.arange(drift_ids.shape[1])
    drifted = jnp.any((mine_ids[None, :] == slots[:, None]) & (slots < count_me)[None, :], axis=1)
    pos = jnp.concatenate([jnp.stack([y, x, core, z]).astype(jnp.int32), drifted.astype(jnp.int32)])

    vmem = pl.BlockSpec(memory_space=pltpu.VMEM)
    smem = pl.BlockSpec(memory_space=pltpu.SMEM)
    big = pltpu.CompilerParams(vmem_limit_bytes=16 << 20)
    x_all = lax.all_gather(x_prompt, "head", axis=0)

    payload = pl.pallas_call(
        payload_kernel,
        out_shape=jax.ShapeDtypeStruct((2 * WROWS + resp_queries.shape[0], width), BF16),
        in_specs=[vmem] * 3,
        out_specs=vmem,
        compiler_params=pltpu.CompilerParams(vmem_limit_bytes=16 << 20),
        name="payload",
    )(key_weight, value_weight, resp_queries)
    near = {a: shift_ctx(payload, dy=-a) for a in (3, 5, 2, 6, 1, 7)}
    near[4] = shift_ctx(near[5], dy=1)
    column, gain = pl.pallas_call(
        column_kernel,
        out_shape=(
            jax.ShapeDtypeStruct((2 * NY + 1, WROWS, width), BF16),
            jax.ShapeDtypeStruct((NZ, slice_width), F32),
        ),
        in_specs=[smem] + [vmem] * (NY + 1),
        out_specs=(vmem, vmem),
        scratch_shapes=[pltpu.VMEM((NY * resp_queries.shape[0], width), F32)],
        compiler_params=pltpu.CompilerParams(vmem_limit_bytes=16 << 20),
        name="column",
    )(pos, payload, *[near[a] for a in range(1, NY)], norm_gain.astype(F32).reshape(NZ, slice_width))

    small = pltpu.CompilerParams(vmem_limit_bytes=8 << 20)

    def part(piece, first, count):
        return pl.pallas_call(
            lambda *refs: part_kernel(first, *refs),
            out_shape=jax.ShapeDtypeStruct((count,) + piece.shape[1:], BF16),
            in_specs=[vmem],
            out_specs=vmem,
            compiler_params=small,
            name="part",
        )(piece)

    following, last = shift_ctx(column, dx=-1), shift_ctx(column, dx=1)
    far_k, far_v = shift_ctx(part(last, 0, NY), dx=1), shift_ctx(part(following, NY, NY + 1), dx=-1)
    own_sw = shift_ctx(column, dcore=1)
    normed, partial, pair = pl.pallas_call(
        project_kernel,
        out_shape=(
            jax.ShapeDtypeStruct((NZ, rows, slice_width), BF16),
            jax.ShapeDtypeStruct((rows, 2 * width), F32),
            jax.ShapeDtypeStruct((2,) + column.shape, BF16),
        ),
        in_specs=[smem] + [vmem] * 6,
        out_specs=(vmem, vmem, vmem),
        compiler_params=big,
        cost_estimate=pl.CostEstimate(flops=3 << 30, bytes_accessed=24 << 20, transcendentals=512),
        name="norm_project",
    )(pos, gain, x_all, column, own_sw, following, last)
    pair_sw = shift_ctx(lax.optimization_barrier((pair, far_k, far_v))[0], dcore=1)
    far = pl.pallas_call(
        join_kernel,
        out_shape=jax.ShapeDtypeStruct(column.shape, BF16),
        in_specs=[vmem] * 2,
        out_specs=vmem,
        compiler_params=small,
        name="join",
    )(far_k, far_v)
    far_sw = shift_ctx(far, dcore=1)

    total = 2 * NY * NX * resp_queries.shape[0]
    result = jax.ShapeDtypeStruct((total // 2, width + 128), BF16)
    new_keys, new_values, packed_mine, packed_other = pl.pallas_call(
        fused_kernel,
        out_shape=(
            jax.ShapeDtypeStruct((rows, width), BF16),
            jax.ShapeDtypeStruct((rows, width), BF16),
            result,
            result,
        ),
        in_specs=[smem] + [vmem] * 12,
        out_specs=(vmem, vmem, vmem, vmem),
        scratch_shapes=[
            pltpu.VMEM((2 * NX, WROWS, width), BF16),
            pltpu.VMEM((rows + 128, width), BF16),
            pltpu.VMEM((rows + 128, width), BF16),
            pltpu.VMEM((rows, 2 * width), F32),
        ],
        compiler_params=big,
        cost_estimate=pl.CostEstimate(flops=3 << 30, bytes_accessed=12 << 20, transcendentals=1 << 20),
        name="refresh_attend",
    )(
        pos,
        cache_keys,
        cache_values,
        resp_keys,
        resp_values,
        normed,
        partial,
        column,
        own_sw,
        pair,
        pair_sw,
        far,
        far_sw,
    )
    merged = pl.pallas_call(
        merge_kernel,
        out_shape=result,
        in_specs=[vmem, vmem],
        out_specs=vmem,
        compiler_params=pltpu.CompilerParams(vmem_limit_bytes=16 << 20),
        name="merge",
    )(packed_mine, shift_ctx(packed_other, dcore=1))
    same = [[(j * NX + i) * 2 + c for i in range(NX) for j in range(NY)] for c in range(2)]
    parts = lax.all_to_all(merged, "ctx", 0, 0, axis_index_groups=same, tiled=True)
    attended = pl.pallas_call(
        combine_kernel,
        out_shape=jax.ShapeDtypeStruct((resp_queries.shape[0], width), BF16),
        in_specs=[vmem],
        out_specs=vmem,
        compiler_params=pltpu.CompilerParams(vmem_limit_bytes=16 << 20),
        name="combine",
    )(parts)
    return new_keys, new_values, attended


def solution(mesh):
    placed = (
        P("ctx", "head"),
        P(),
        P("ctx", "head"),
        P("ctx", "head"),
        P("ctx", "head"),
        P("ctx", "head"),
        P("ctx", "head"),
        P("ctx", "head"),
        P("ctx", "head"),
        P(),
        P(),
    )
    return jax.shard_map(
        body,
        mesh=mesh,
        in_specs=placed,
        out_specs=(P("ctx", "head"), P("ctx", "head"), P("ctx", "head")),
        check_vma=False,
    )
```
